32 devices in a mesh: row: 8 (over z, core), col: 4 (over y, x).
Axes of the slice: x: 2, y: 2, z: 4, core: 2. Of those that a mesh axis runs over, the one named last changes fastest.
Arguments:
- tensor: float32 [16, 2048, 1024], P(None, 'row', 'col'), may hold values from -270 to 270
- factor_b: float32 [64, 1024], P(None, 'col'), may hold values from -6 to 6
- factor_c: float32 [16, 64], replicated, may hold values from -6 to 6
Outputs:
- result_a: float32 [64, 2048], P(None, 'row')
- result_b: float32 [64, 1024], P(None, 'col')
- column_scales: float32 [2, 64], replicated
The draws below stay inside these ranges and needn't reach their ends.
All inputs are finite; a program needn't handle non-finite values.
Results may differ from the reference program's by a relative error of at most 0.0003.
Values sent between devices are 32-bit elements; how exact they have to be, the bound alone decides.
No kernel may reach another device: no remote copies, remote signals or barrier semaphores. Data moves between devices by JAX's collectives and lax.ppermute only.
A program may use at most 64 MiB of HBM per device.

```python
import math
import jax
import jax.numpy as jnp
from jax import lax

K = 16
R = 64
SWEEPS = 3
NI = 2048
NJ = 1024


def draw_tensor(key, part):
    key = jax.random.fold_in(key, 1)
    key_row, key_col, key_noise = jax.random.split(key, 3)
    row_pos = jnp.arange(NI, dtype=jnp.float32) / NI
    col_pos = jnp.arange(NJ, dtype=jnp.float32) / NJ
    row_scale = (1.0 + 2.0 * row_pos) * jnp.exp(jax.random.uniform(key_row, (NI,), jnp.float32, 0.0, math.log(10.0)))
    col_scale = (1.0 + 2.0 * col_pos) * jnp.exp(jax.random.uniform(key_col, (NJ,), jnp.float32, 0.0, math.log(10.0)))
    noise = jnp.clip(jax.random.normal(key_noise, (K, NI, NJ), jnp.float32), -6.0, 6.0)
    return (0.05 * noise * row_scale[None, :, None] * col_scale[None, None, :]).astype(jnp.float32)


def shard_levels(own_key, shape, shards, smallest, high):
    factor_of, own = 1.0, jax.random.fold_in(own_key, 6)
    for position, blocks in shards:
        heights = jnp.exp(jax.random.uniform(jax.random.fold_in(own, position), (blocks,), jnp.float32, smallest / len(shards), high / len(shards)))
        factor_of = factor_of * jnp.repeat(heights, shape[position] // blocks).reshape([-1 if axis == position else 1 for axis in range(len(shape))])
    return factor_of


def normal_values(key, extent, width, limit, cuts=(), kind=jnp.bfloat16):
    gain = shard_levels(key, extent, cuts, -0.22, 0.18) if cuts else 1.0
    drawn = jax.random.normal(key, extent, jnp.float32) * width * gain
    return jnp.minimum(jnp.maximum(drawn, -limit), limit).astype(kind)


def setup_inputs(seed: int = 0) -> dict:
    keys = jax.random.split(jax.random.key(seed), 4)
    return {
        "tensor": draw_tensor(jax.random.fold_in(keys[3], 71), 0),
        "factor_b": normal_values(keys[1], (R, NJ), 1.0, 6.0, ((1, 4),), jnp.float32),
        "factor_c": normal_values(keys[2], (K, R), 1.0, 6.0, (), jnp.float32),
    }


epsilon = 1e-06

def gram_of(factor):
    return jnp.dot(factor.astype(jnp.float32), factor.T.astype(jnp.float32), precision=lax.Precision.HIGHEST, preferred_element_type=jnp.float32)

def update(mttkrp, system, count):
    lower = jnp.linalg.cholesky(system)
    solved = jax.scipy.linalg.cho_solve((lower, True), mttkrp)
    scales = jnp.sqrt(lax.optimization_barrier(jnp.sum(solved * solved, axis=1)) / count + epsilon)
    return (solved / scales[:, None], scales)

def reference(tensor, factor_b, factor_c):
    highest = lax.Precision.HIGHEST
    identity = jnp.eye(R, dtype=jnp.float32)
    gram_c = jnp.dot(factor_c.T.astype(jnp.float32), factor_c.astype(jnp.float32), precision=highest, preferred_element_type=jnp.float32)
    current_b = factor_b
    gram_b = gram_of(current_b)
    current_a = jnp.zeros((R, NI), jnp.float32)
    scales_a = jnp.zeros((R,), jnp.float32)
    scales_b = jnp.zeros((R,), jnp.float32)
    for sweep in range(SWEEPS):
        inner = jnp.einsum('kij,rj->kir', tensor, current_b, precision=highest)
        mttkrp_a = jnp.einsum('kir,kr->ri', inner, factor_c, precision=highest)
        current_a, scales_a = update(mttkrp_a, gram_c * gram_b + NJ * identity, NI)
        gram_a = gram_of(current_a)
        outer = jnp.einsum('ri,kij->krj', current_a, tensor, precision=highest)
        mttkrp_b = jnp.einsum('krj,kr->rj', outer, factor_c, precision=highest)
        current_b, scales_b = update(mttkrp_b, gram_c * gram_a + NI * identity, NJ)
        gram_b = gram_of(current_b)
    return (current_a, current_b, jnp.stack([scales_a, scales_b]))
```

```python
import functools

import jax
import jax.numpy as jnp
from jax import lax
from jax.experimental import pallas as pl
from jax.experimental.pallas import tpu as pltpu
from jax.sharding import PartitionSpec as P

SWEEPS = 3
EPSILON = 1e-06
TOLERANCE = 2e-06
RELAX = 0.95
VMEM_LIMIT = 16 * 1024 * 1024


def dot(x, y, contract=(1, 0), precision=None):
    return lax.dot_general(
        x,
        y,
        (((contract[0],), (contract[1],)), ((), ())),
        precision=precision,
        preferred_element_type=jnp.float32,
    )


exact_dot = functools.partial(dot, precision=lax.Precision.HIGHEST)


def split(x):
    high = x.astype(jnp.bfloat16)
    return high, (x - high.astype(jnp.float32)).astype(jnp.bfloat16)


def split_dot(x, y, contract=(1, 0)):
    rows = x[0].shape[0]
    both = dot(jnp.concatenate(x, axis=0), y[0], contract)
    return both[:rows] + (both[rows:] + dot(x[0], y[1], contract))


def identity_mask(rank):
    rows = lax.broadcasted_iota(jnp.int32, (rank, rank), 0)
    return rows == lax.broadcasted_iota(jnp.int32, (rank, rank), 1)


def groups(depth):
    ends = list(range(4, depth - 3, 4)) + list(range(max(depth - 2, 1), depth + 1, 2))
    return [range(start, end) for start, end in zip([0] + ends, ends)]


def mttkrp(factor, columns_c, high_ref, low_ref, ready=None):
    rank = factor.shape[0]
    both, cross = None, None
    for k in range(high_ref.shape[0]):
        if ready is not None:
            ready(k)
        high, low = split(factor * columns_c[:, k : k + 1])
        first = dot(jnp.concatenate([high, low], axis=0), high_ref[k])
        second = dot(high, low_ref[k])
        both = first if both is None else both + first
        cross = second if cross is None else cross + second
    return both[:rank] + (both[rank:] + cross)


def pack_gram(gram, width):
    rank = gram.shape[0]
    parts = width // rank
    rows = rank // parts
    return jnp.concatenate([gram[q * rows : (q + 1) * rows] for q in range(parts)], axis=1)


def unpack_gram(packed, rank):
    parts = packed.shape[1] // rank
    return jnp.concatenate([packed[:, q * rank : (q + 1) * rank] for q in range(parts)], axis=0)


def tree_sum(pieces):
    pieces = list(pieces)
    while len(pieces) > 1:
        pieces = [pieces[i] + pieces[i + 1] for i in range(0, len(pieces), 2)]
    return pieces[0]


def scale_system(gram_c, gram, mask, count, normalized):
    if normalized:
        system = gram_c * gram + jnp.where(mask, gram + count * EPSILON, 0.0)
    else:
        system = gram_c * gram + jnp.where(mask, jnp.float32(count), 0.0)
    diagonal = jnp.where(mask, system, 0.0)
    row, column = [jnp.sum(diagonal, axis=axis, keepdims=True) for axis in (0, 1)]
    error = jnp.where(mask, 1.0 - RELAX, -system * (RELAX / row))
    return error, row, column


def series(error, rhs, doublings):
    power = error
    for step in range(doublings - 1):
        parts = split(power)
        rhs = rhs + split_dot(parts, split(rhs))
        power = split_dot(parts, parts) if step < doublings - 2 else dot(parts[0], parts[0])
    return rhs + dot(power.astype(jnp.bfloat16), rhs.astype(jnp.bfloat16)), power


def careful_inverse(error, mask, total_ref, power_ref):
    unit = jnp.where(mask, 1.0, 0.0)
    system = unit - error
    bound = jnp.max(jnp.sum(jnp.abs(system), axis=0, keepdims=True), axis=1, keepdims=True)
    omega = jnp.minimum(1.0, 1.9 / bound)
    power = unit - omega * system
    total_ref[...] = unit + power
    power_ref[...] = power

    def unfinished(state):
        step, rest = state
        return jnp.logical_and(step < 48, rest > 1e-7)

    def double(state):
        power = exact_dot(power_ref[...], power_ref[...])
        power_ref[...] = power
        total = total_ref[...]
        total_ref[...] = total + exact_dot(total, power)
        return state[0] + 1, jnp.sum(power * power)

    lax.while_loop(unfinished, double, (jnp.int32(0), jnp.float32(1.0)))
    return omega * total_ref[...]


def start_kernel(tensor_hbm, factor_hbm, c_hbm, high_ref, low_ref, turned_high_ref, turned_low_ref, *refs):
    gram_c_ref, columns_ref, out_ref, tensor_ref, factor_ref, c_ref, padded_ref, sems = refs
    depth, rank = c_hbm.shape
    small = [
        pltpu.make_async_copy(c_hbm, c_ref, sems.at[depth]),
        pltpu.make_async_copy(factor_hbm, factor_ref, sems.at[depth + 1]),
    ]
    slices = {}
    for group in groups(depth):
        some = pl.ds(group[0], len(group))
        slices[group[0]] = pltpu.make_async_copy(tensor_hbm.at[some], tensor_ref.at[some], sems.at[group[0]])
    for copy in small + list(slices.values()):
        copy.start()
    for copy in small:
        copy.wait()
    padded_ref[:depth, :rank] = c_ref[...]
    columns_c = padded_ref[...].T[:rank, :depth]
    columns_ref[...] = columns_c
    factor = factor_ref[...]

    def ready(k):
        if k == groups(depth)[-1][0]:
            gram_c_ref[...] = exact_dot(columns_c, columns_c, (1, 1))
            parts = split(factor)
            out_ref[rank:] = pack_gram(split_dot(parts, parts, (1, 1)), factor.shape[1])
        if k in slices:
            slices[k].wait()
        high, low = split(tensor_ref[k])
        high_ref[k], low_ref[k] = high, low
        turned_high_ref[k], turned_low_ref[k] = high.T, low.T

    out_ref[:rank] = mttkrp(factor, columns_c, turned_high_ref, turned_low_ref, ready)


def own_core():
    return lax.axis_index("row") % 2


def own_half(rows):
    return pl.ds(pl.multiple_of(own_core() * (rows // 2), 8), rows // 2)


def merge(sum_ref, trade_refs, full_ref):
    if len(trade_refs) < 3:
        return tree_sum([ref[...] for ref in (sum_ref, *trade_refs)])
    got_ref, half_ref, swapped_ref = trade_refs
    rows = sum_ref.shape[0]
    core = own_core()
    full_ref[core] = got_ref[...]
    full_ref[1 - core] = swapped_ref[:rows]
    full_ref[2, own_half(rows)] = half_ref[...]
    full_ref[2, pl.ds(pl.multiple_of((1 - core) * (rows // 2), 8), rows // 2)] = swapped_ref[rows:]
    return (sum_ref[...] + full_ref[0]) + (full_ref[1] + full_ref[2])


def merge_kernel(count, sum_ref, *refs):
    trade_refs, (out_ref, half_ref, full_ref) = refs[:count], refs[count:]
    out_ref[...] = merge(sum_ref, trade_refs, full_ref)
    half_ref[...] = out_ref[own_half(out_ref.shape[0])]


def solve_kernel(count, normalized, summed, gram_c_ref, columns_ref, high_ref, low_ref, refs, scratch):
    rank = gram_c_ref.shape[0]
    mask = identity_mask(rank)
    gram = unpack_gram(summed[rank:], rank)
    error, row, column = scale_system(gram_c_ref[...], gram, mask, count, normalized)
    outer = RELAX / column
    if normalized:
        diagonal = jnp.where(mask, gram, 0.0)
        scales = [jnp.sqrt(jnp.sum(diagonal, axis=axis, keepdims=True) / count + EPSILON) for axis in (0, 1)]
        outer = outer * scales[1]
    packed_ref, solved_ref, squares_ref, scales_ref = refs
    if scales_ref is not None:
        scales_ref[...] = scales[0]

    def emit(solved):
        if solved_ref is not None:
            solved_ref[...] = solved
        if squares_ref is not None:
            squares = jnp.sum(solved * solved, axis=1, keepdims=True)
            row = jnp.sum(jnp.where(mask, squares, 0.0), axis=0, keepdims=True)
            squares_ref[...] = jnp.concatenate([row, row], axis=1) * jnp.ones((8, 1), jnp.float32)
        if packed_ref is not None:
            parts = split(solved)
            packed_ref[rank:] = pack_gram(split_dot(parts, parts, (1, 1)), solved.shape[1])
            packed_ref[:rank] = mttkrp(solved, columns_ref[...], high_ref, low_ref)

    solved, power = series(error, summed[:rank], 4)
    emit(outer * solved)
    roots = 1.0 / jnp.sqrt(column), jnp.sqrt(row)
    rest = jnp.sum(jnp.square(power * roots[0] * roots[1]))

    @pl.when(jnp.logical_not(rest <= TOLERANCE))
    def _():
        symmetric = error * roots[0] * roots[1]
        inverse = careful_inverse(symmetric, mask, *scratch)
        emit(outer / roots[0] * exact_dot(inverse, roots[0] * summed[:rank]))


def left_kernel(pieces_count, count, normalized, last, *refs):
    pieces, refs = refs[:pieces_count], refs[pieces_count:]
    parts, (packed_ref, *solved_ref), scratch = refs[:4], refs[4:-2], refs[-2:]
    summed = tree_sum([ref[...] for ref in pieces])
    outs = (packed_ref, solved_ref[0] if last else None, None, None)
    solve_kernel(count, normalized, summed, *parts, outs, scratch)


def right_kernel(pieces_count, count, last, sum_ref, *refs):
    pieces, refs = refs[:pieces_count], refs[pieces_count:]
    parts, outs, (full_ref, *scratch) = refs[:4], refs[4:-3], refs[-3:]
    outs = (None, *outs) if last else (*outs, None, None, None)
    solve_kernel(count, True, merge(sum_ref, pieces, full_ref), *parts, outs, scratch)


def finish_kernel(pieces_count, count, *refs):
    pieces, refs = refs[:pieces_count], refs[pieces_count:]
    scales_a_ref, solved_a_ref, solved_b_ref, result_a_ref, result_b_ref, scales_ref = refs
    rank = solved_b_ref.shape[0]
    mask = identity_mask(rank)
    row_b = jnp.sqrt(tree_sum([ref[...] for ref in pieces])[0:1, :rank] / count + EPSILON)
    row_a = scales_a_ref[...]
    column_a, column_b = [jnp.sum(jnp.where(mask, row, 0.0), axis=1, keepdims=True) for row in (row_a, row_b)]
    result_a_ref[...] = solved_a_ref[...] / column_a
    result_b_ref[...] = solved_b_ref[...] / column_b
    scales_ref[...] = jnp.concatenate([row_a, row_b], axis=0)


def call(kernel, out_shape, *args, scratch=(), **options):
    return pl.pallas_call(
        kernel,
        out_shape=out_shape,
        scratch_shapes=scratch,
        compiler_params=pltpu.CompilerParams(vmem_limit_bytes=VMEM_LIMIT),
        **options,
    )(*args)


def swap(x, axis, stride):
    return lax.ppermute(x, axis, [(d, d ^ stride) for d in range(lax.axis_size(axis))])


def exchange(x, axis, stride=1, radix=4):
    size = lax.axis_size(axis)
    while True:
        group = min(radix, size // stride)
        order = (1, 3, 2) if group == 4 else range(1, group)
        got = {m: swap(x, axis, m * stride) for m in order}
        pieces = [x] + [got[m] for m in range(1, group)]
        stride *= group
        if stride >= size:
            return pieces
        x = tree_sum(pieces)


def exchange_by_cores(x, axis):
    size = lax.axis_size(axis)
    half = jax.ShapeDtypeStruct((x.shape[0] // 2, x.shape[1]), x.dtype)
    scratch = [pltpu.VMEM((3,) + x.shape, x.dtype)]
    stride, trades = 2, (swap(x, axis, 1),)
    while stride < size:
        x, own = call(functools.partial(merge_kernel, len(trades)), (x, half), x, *trades, scratch=scratch)
        if 2 * stride < size:
            pairs = [(d, d ^ (stride if d % 2 == 0 else 2 * stride)) for d in range(size)]
            half_got = swap(own, axis, 3 * stride)
            got = lax.ppermute(x, axis, pairs)
            trades = (got, half_got, swap(jnp.concatenate([got, half_got], axis=0), axis, 1))
        else:
            trades = (swap(x, axis, stride),)
        stride *= 4
    return x, trades


def shards(tensor, factor_b, factor_c):
    rows_all = tensor.shape[1] * lax.axis_size("row")
    cols_all = tensor.shape[2] * lax.axis_size("col")
    depth, height, width = tensor.shape
    rank = factor_c.shape[1]
    f32 = functools.partial(jax.ShapeDtypeStruct, dtype=jnp.float32)
    part = jax.ShapeDtypeStruct(tensor.shape, jnp.bfloat16)
    turned = jax.ShapeDtypeStruct((depth, width, height), jnp.bfloat16)
    left, right = (rank, height), (rank, width)
    packed_a, packed_b = [(rank + rank * rank // n, n) for n in (height, width)]
    inverse = [pltpu.VMEM((rank, rank), jnp.float32)] * 2
    scratch = [pltpu.VMEM((3,) + packed_b, jnp.float32)] + inverse
    high, low, turned_high, turned_low, gram_c, columns, partial = call(
        start_kernel,
        (part, part, turned, turned, f32((rank, rank)), f32((rank, depth)), f32(packed_a)),
        *[pltpu.with_memory_space_constraint(x, pltpu.HBM) for x in (tensor, factor_b, factor_c)],
        in_specs=[pl.BlockSpec(memory_space=pltpu.HBM)] * 3,
        scratch=[
            pltpu.VMEM(tensor.shape, jnp.float32),
            pltpu.VMEM(factor_b.shape, jnp.float32),
            pltpu.VMEM(factor_c.shape, jnp.float32),
            pltpu.VMEM((128, 128), jnp.float32),
            pltpu.SemaphoreType.DMA((depth + 2,)),
        ],
    )
    parts, turned_parts = (gram_c, columns, high, low), (gram_c, columns, turned_high, turned_low)
    for sweep in range(SWEEPS):
        last = sweep == SWEEPS - 1
        pieces = exchange(partial, "col")
        kernel = functools.partial(left_kernel, len(pieces), cols_all, sweep > 0, last)
        outs = (f32(packed_b), f32(left)) if last else (f32(packed_b),)
        partial, *solved_a = call(kernel, outs, *pieces, *parts, scratch=inverse)
        partial, pieces = exchange_by_cores(partial, "row")
        kernel = functools.partial(right_kernel, len(pieces), rows_all, last)
        outs = (f32(right), f32((8, 2 * rank)), f32((1, rank))) if last else (f32(packed_a),)
        partial, *rest = call(kernel, outs, partial, *pieces, *turned_parts, scratch=scratch)
    solved_b, (squares, scales_a) = partial, rest
    pieces = exchange(squares, "col")
    kernel = functools.partial(finish_kernel, len(pieces), cols_all)
    outs = (f32(left), f32(right), f32((2, rank)))
    return tuple(call(kernel, outs, *pieces, scales_a, *solved_a, solved_b))


def solution(mesh):
    in_specs = (P(None, "row", "col"), P(None, "col"), P())
    out_specs = (P(None, "row"), P(None, "col"), P())
    return jax.shard_map(shards, mesh=mesh, in_specs=in_specs, out_specs=out_specs, check_vma=False)
```

```python
import functools

import jax
import jax.numpy as jnp
from jax import lax
from jax.experimental import pallas as pl
from jax.experimental.pallas import tpu as pltpu
from jax.sharding import PartitionSpec as P

SWEEPS = 3
EPSILON = 1e-06
TOLERANCE = 2e-06
RELAX = 0.95
GROUP = 4
VMEM_LIMIT = 16 * 1024 * 1024


def dot(x, y, contract=(1, 0), precision=None):
    return lax.dot_general(
        x,
        y,
        (((contract[0],), (contract[1],)), ((), ())),
        precision=precision,
        preferred_element_type=jnp.float32,
    )


exact_dot = functools.partial(dot, precision=lax.Precision.HIGHEST)


def split(x):
    high = x.astype(jnp.bfloat16)
    return high, (x - high.astype(jnp.float32)).astype(jnp.bfloat16)


def split_dot(x, y, contract=(1, 0)):
    rows = x[0].shape[0]
    both = dot(jnp.concatenate(x, axis=0), y[0], contract)
    return both[:rows] + (both[rows:] + dot(x[0], y[1], contract))


def identity_mask(rank):
    rows = lax.broadcasted_iota(jnp.int32, (rank, rank), 0)
    return rows == lax.broadcasted_iota(jnp.int32, (rank, rank), 1)


def mttkrp(factor, columns_c, high_ref, low_ref, ready=None):
    rank = factor.shape[0]
    both, cross = None, None
    for k in range(high_ref.shape[0]):
        if ready is not None:
            ready(k)
        high, low = split(factor * columns_c[:, k : k + 1])
        first = dot(jnp.concatenate([high, low], axis=0), high_ref[k])
        second = dot(high, low_ref[k])
        both = first if both is None else both + first
        cross = second if cross is None else cross + second
    return both[:rank] + (both[rank:] + cross)


def pack_gram(gram, width):
    rank = gram.shape[0]
    parts = width // rank
    rows = rank // parts
    return jnp.concatenate([gram[q * rows : (q + 1) * rows] for q in range(parts)], axis=1)


def pack(solved, columns_ref, high_ref, low_ref, packed_ref):
    rank, width = solved.shape
    parts = split(solved)
    packed_ref[rank:] = pack_gram(split_dot(parts, parts, (1, 1)), width)
    packed_ref[:rank] = mttkrp(solved, columns_ref[...], high_ref, low_ref)


def unpack_gram(packed, rank):
    parts = packed.shape[1] // rank
    return jnp.concatenate([packed[:, q * rank : (q + 1) * rank] for q in range(parts)], axis=0)


def tree_sum(pieces):
    pieces = list(pieces)
    while len(pieces) > 1:
        pieces = [pieces[i] + pieces[i + 1] for i in range(0, len(pieces), 2)]
    return pieces[0]


def scale_system(gram_c, gram, mask, count, normalized):
    if normalized:
        system = gram_c * gram + jnp.where(mask, gram + count * EPSILON, 0.0)
    else:
        system = gram_c * gram + jnp.where(mask, jnp.float32(count), 0.0)
    diagonal = jnp.where(mask, system, 0.0)
    row, column = [jnp.sum(diagonal, axis=axis, keepdims=True) for axis in (0, 1)]
    error = jnp.where(mask, 1.0 - RELAX, -system * (RELAX / row))
    return error, row, column


def series(error, rhs, doublings):
    power = error
    for step in range(doublings - 1):
        parts = split(power)
        rhs = rhs + split_dot(parts, split(rhs))
        power = split_dot(parts, parts) if step < doublings - 2 else dot(parts[0], parts[0])
    return rhs + dot(power.astype(jnp.bfloat16), rhs.astype(jnp.bfloat16)), power


def inverse_series(error, mask, doublings):
    total, power = jnp.where(mask, 1.0, 0.0) + error, error
    for step in range(doublings - 1):
        parts = split(power)
        power = split_dot(parts, parts) if step < doublings - 2 else dot(parts[0], parts[0])
        total = total + split_dot(split(power), split(total))
    return total, power


def careful_inverse(error, mask, total_ref, power_ref):
    unit = jnp.where(mask, 1.0, 0.0)
    system = unit - error
    bound = jnp.max(jnp.sum(jnp.abs(system), axis=0, keepdims=True), axis=1, keepdims=True)
    omega = jnp.minimum(1.0, 1.9 / bound)
    power = unit - omega * system
    total_ref[...] = unit + power
    power_ref[...] = power

    def unfinished(state):
        step, rest = state
        return jnp.logical_and(step < 48, rest > 1e-7)

    def double(state):
        power = exact_dot(power_ref[...], power_ref[...])
        power_ref[...] = power
        total = total_ref[...]
        total_ref[...] = total + exact_dot(total, power)
        return state[0] + 1, jnp.sum(power * power)

    lax.while_loop(unfinished, double, (jnp.int32(0), jnp.float32(1.0)))
    return omega * total_ref[...]


def start_kernel(tensor_hbm, factor_hbm, c_hbm, high_ref, low_ref, turned_high_ref, turned_low_ref, *refs):
    gram_c_ref, columns_ref, out_ref, tensor_ref, factor_ref, c_ref, padded_ref, sems = refs
    depth, rank = c_hbm.shape
    small = [
        pltpu.make_async_copy(c_hbm, c_ref, sems.at[depth]),
        pltpu.make_async_copy(factor_hbm, factor_ref, sems.at[depth + 1]),
    ]
    slices = []
    for k in range(0, depth, GROUP):
        some = pl.ds(k, min(GROUP, depth - k))
        slices.append(pltpu.make_async_copy(tensor_hbm.at[some], tensor_ref.at[some], sems.at[k]))
    for copy in small + slices:
        copy.start()
    for copy in small:
        copy.wait()
    padded_ref[:depth, :rank] = c_ref[...]
    columns_c = padded_ref[...].T[:rank, :depth]
    columns_ref[...] = columns_c
    factor = factor_ref[...]

    def arrive(k):
        if k % GROUP == 0 and k < depth:
            slices[k // GROUP].wait()
            for k in range(k, min(k + GROUP, depth)):
                high, low = split(tensor_ref[k])
                high_ref[k], low_ref[k] = high, low
                turned_high_ref[k], turned_low_ref[k] = high.T, low.T

    def ready(k):
        if k == 0:
            arrive(0)
        arrive(k + GROUP)
        if k == GROUP:
            gram_c_ref[...] = exact_dot(columns_c, columns_c, (1, 1))
            parts = split(factor)
            out_ref[rank:] = pack_gram(split_dot(parts, parts, (1, 1)), factor.shape[1])

    out_ref[:rank] = mttkrp(factor, columns_c, turned_high_ref, turned_low_ref, ready)


def own_core():
    return lax.axis_index("row") % 2


def own_half(rows, core):
    return pl.ds(pl.multiple_of(core * (rows // 2), 8), rows // 2)


def traded_gram(rank, sum_ref, got_ref, half_ref, swapped_ref):
    here, got, swapped = [ref[rank:] for ref in (sum_ref, got_ref, swapped_ref)]
    first = own_core() == 0
    return (here + jnp.where(first, got, swapped)) + (jnp.where(first, swapped, got) + half_ref[rank // 2 :])


def traded_sum(rank, sum_ref, got_ref, half_ref, swapped_ref, other_ref, full_ref):
    core = own_core()
    full_ref[core] = got_ref[:rank]
    full_ref[1 - core] = swapped_ref[:rank]
    full_ref[2, own_half(rank, core)] = half_ref[: rank // 2]
    full_ref[2, own_half(rank, 1 - core)] = other_ref[...]
    return (sum_ref[:rank] + full_ref[0]) + (full_ref[1] + full_ref[2])


def merge_kernel(rank, *refs):
    pieces, (out_ref, half_ref, full_ref) = refs[:-3], refs[-3:]
    if len(pieces) == 2:
        out_ref[...] = pieces[0][...] + pieces[1][...]
    else:
        out_ref[rank:] = traded_gram(rank, *pieces[:4])
        out_ref[:rank] = traded_sum(rank, *pieces, full_ref)
    half_ref[: rank // 2] = out_ref[own_half(rank, own_core())]
    half_ref[rank // 2 :] = out_ref[rank:]


def factor_scales(gram, mask, count):
    diagonal = jnp.where(mask, gram, 0.0)
    return [jnp.sqrt(jnp.sum(diagonal, axis=axis, keepdims=True) / count + EPSILON) for axis in (0, 1)]


def invert_kernel(count, *refs):
    trades, (gram_c_ref, inverse_ref, *scales_ref), scratch = refs[:4], refs[4:-2], refs[-2:]
    rank = gram_c_ref.shape[0]
    mask = identity_mask(rank)
    gram = unpack_gram(traded_gram(rank, *trades), rank)
    error, row, column = scale_system(gram_c_ref[...], gram, mask, count, True)
    scales = factor_scales(gram, mask, count)
    if scales_ref:
        scales_ref[0][...] = scales[0]
    outer = RELAX * scales[1] / column
    total, power = inverse_series(error, mask, 4)
    inverse_ref[...] = outer * total
    roots = 1.0 / jnp.sqrt(column), jnp.sqrt(row)
    rest = jnp.sum(jnp.square(power * roots[0] * roots[1]))

    @pl.when(jnp.logical_not(rest <= TOLERANCE))
    def _():
        symmetric = error * roots[0] * roots[1]
        inverse_ref[...] = (outer / roots[0]) * careful_inverse(symmetric, mask, *scratch) / roots[1]


def left_kernel(pieces_count, count, normalized, last, *refs):
    pieces, refs = refs[:pieces_count], refs[pieces_count:]
    (gram_c_ref, *parts), (packed_ref, *solved_ref), scratch = refs[:4], refs[4:-2], refs[-2:]
    rank = gram_c_ref.shape[0]
    mask = identity_mask(rank)
    summed = tree_sum([ref[...] for ref in pieces])
    gram = unpack_gram(summed[rank:], rank)
    error, row, column = scale_system(gram_c_ref[...], gram, mask, count, normalized)
    outer = RELAX / column
    if normalized:
        outer = outer * factor_scales(gram, mask, count)[1]

    def emit(solved):
        if last:
            solved_ref[0][...] = solved
        pack(solved, *parts, packed_ref)

    solved, power = series(error, summed[:rank], 4)
    emit(outer * solved)
    roots = 1.0 / jnp.sqrt(column), jnp.sqrt(row)
    rest = jnp.sum(jnp.square(power * roots[0] * roots[1]))

    @pl.when(jnp.logical_not(rest <= TOLERANCE))
    def _():
        symmetric = error * roots[0] * roots[1]
        inverse = careful_inverse(symmetric, mask, *scratch)
        emit(outer / roots[0] * exact_dot(inverse, roots[0] * summed[:rank]))


def right_kernel(last, *refs):
    trades, inverse_ref, refs, full_ref = refs[:5], refs[5], refs[6:-1], refs[-1]
    rank = inverse_ref.shape[0]
    solved = split_dot(split(inverse_ref[...]), split(traded_sum(rank, *trades, full_ref)))
    if last:
        solved_ref, squares_ref = refs
        solved_ref[...] = solved
        squares = jnp.sum(solved * solved, axis=1, keepdims=True)
        row = jnp.sum(jnp.where(identity_mask(rank), squares, 0.0), axis=0, keepdims=True)
        squares_ref[...] = jnp.concatenate([row, row], axis=1) * jnp.ones((8, 1), jnp.float32)
    else:
        pack(solved, *refs)


def result_kernel(scales_ref, solved_ref, result_ref, out_ref):
    row = scales_ref[...]
    mask = identity_mask(row.shape[1])
    result_ref[...] = solved_ref[...] / jnp.sum(jnp.where(mask, row, 0.0), axis=1, keepdims=True)
    out_ref[...] = row


def finish_kernel(pieces_count, count, *refs):
    pieces, (scales_a_ref, solved_ref, result_ref, scales_ref) = refs[:pieces_count], refs[pieces_count:]
    rank = solved_ref.shape[0]
    row = jnp.sqrt(tree_sum([ref[...] for ref in pieces])[0:1, :rank] / count + EPSILON)
    result_ref[...] = solved_ref[...] / jnp.sum(jnp.where(identity_mask(rank), row, 0.0), axis=1, keepdims=True)
    scales_ref[...] = jnp.concatenate([scales_a_ref[...], row], axis=0)


def call(kernel, out_shape, *args, scratch=(), **options):
    return pl.pallas_call(
        kernel,
        out_shape=out_shape,
        scratch_shapes=scratch,
        compiler_params=pltpu.CompilerParams(vmem_limit_bytes=VMEM_LIMIT),
        **options,
    )(*args)


def swap(x, axis, stride):
    return lax.ppermute(x, axis, [(d, d ^ stride) for d in range(lax.axis_size(axis))])


def exchange(x, axis, stride=1, radix=4):
    size = lax.axis_size(axis)
    while True:
        group = min(radix, size // stride)
        pieces = [x] + [swap(x, axis, m * stride) for m in range(1, group)]
        stride *= group
        if stride >= size:
            return pieces
        x = tree_sum(pieces)


def exchange_by_cores(x, axis, rank):
    size = lax.axis_size(axis)
    out = jax.ShapeDtypeStruct((x.shape[0] - rank // 2, x.shape[1]), x.dtype)
    scratch = [pltpu.VMEM((3, rank, x.shape[1]), x.dtype)]
    stride, pieces = 2, (x, swap(x, axis, 1))
    while stride < size:
        x, own = call(functools.partial(merge_kernel, rank), (x, out), *pieces, scratch=scratch)
        half = swap(own, axis, 3 * stride)
        got = lax.ppermute(x, axis, [(d, d ^ (stride if d % 2 == 0 else 2 * stride)) for d in range(size)])
        pieces = (x, got, half, swap(got, axis, 1), swap(half[: rank // 2], axis, 1))
        stride *= 4
    return pieces


def shards(tensor, factor_b, factor_c):
    rows_all = tensor.shape[1] * lax.axis_size("row")
    cols_all = tensor.shape[2] * lax.axis_size("col")
    depth, height, width = tensor.shape
    rank = factor_c.shape[1]
    f32 = functools.partial(jax.ShapeDtypeStruct, dtype=jnp.float32)
    part = jax.ShapeDtypeStruct(tensor.shape, jnp.bfloat16)
    turned = jax.ShapeDtypeStruct((depth, width, height), jnp.bfloat16)
    left, right = (rank, height), (rank, width)
    packed_a, packed_b = [(rank + rank * rank // n, n) for n in (height, width)]
    scratch = [pltpu.VMEM((rank, rank), jnp.float32)] * 2
    full = [pltpu.VMEM((3, rank, width), jnp.float32)]
    high, low, turned_high, turned_low, gram_c, columns, partial = call(
        start_kernel,
        (part, part, turned, turned, f32((rank, rank)), f32((rank, depth)), f32(packed_a)),
        *[pltpu.with_memory_space_constraint(x, pltpu.HBM) for x in (tensor, factor_b, factor_c)],
        in_specs=[pl.BlockSpec(memory_space=pltpu.HBM)] * 3,
        scratch=[
            pltpu.VMEM(tensor.shape, jnp.float32),
            pltpu.VMEM(factor_b.shape, jnp.float32),
            pltpu.VMEM(factor_c.shape, jnp.float32),
            pltpu.VMEM((128, 128), jnp.float32),
            pltpu.SemaphoreType.DMA((depth + 2,)),
        ],
    )
    cost = pl.CostEstimate(flops=0, bytes_accessed=4 * tensor.size, transcendentals=0)
    for sweep in range(SWEEPS):
        last = sweep == SWEEPS - 1
        pieces = exchange(partial, "col")
        kernel = functools.partial(left_kernel, len(pieces), cols_all, sweep > 0, last)
        outs = (f32(packed_b), f32(left)) if last else (f32(packed_b),)
        partial, *solved_a = call(kernel, outs, *pieces, gram_c, columns, high, low, scratch=scratch)
        pieces = exchange_by_cores(partial, "row", rank)
        kernel = functools.partial(invert_kernel, rows_all)
        outs = (f32((rank, rank)), f32((1, rank))) if last else (f32((rank, rank)),)
        inverse, *scales_a = call(kernel, outs, *pieces[:4], gram_c, scratch=scratch, cost_estimate=cost)
        kernel = functools.partial(right_kernel, last)
        if not last:
            partial = call(
                kernel, f32(packed_a), *pieces, inverse, columns, turned_high, turned_low, scratch=full
            )
        else:
            solved_b, squares = call(kernel, (f32(right), f32((8, 2 * rank))), *pieces, inverse, scratch=full)
    pieces = exchange(squares, "col")
    result_a, scales_a = call(result_kernel, (f32(left), f32((1, rank))), *scales_a, *solved_a, cost_estimate=cost)
    kernel = functools.partial(finish_kernel, len(pieces), cols_all)
    result_b, scales = call(kernel, (f32(right), f32((2, rank))), *pieces, scales_a, solved_b)
    return result_a, result_b, scales


def solution(mesh):
    in_specs = (P(None, "row", "col"), P(None, "col"), P())
    out_specs = (P(None, "row"), P(None, "col"), P())
    return jax.shard_map(shards, mesh=mesh, in_specs=in_specs, out_specs=out_specs, check_vma=False)
```

```python
import functools

import jax
import jax.numpy as jnp
from jax import lax
from jax.experimental import pallas as pl
from jax.experimental.pallas import tpu as pltpu
from jax.sharding import PartitionSpec as P

SWEEPS = 3
EPSILON = 1e-06
TOLERANCE = 2e-06
RELAX = 0.95
GROUP = 4
VMEM_LIMIT = 16 * 1024 * 1024


def dot(x, y, contract=(1, 0), precision=None):
    return lax.dot_general(
        x,
        y,
        (((contract[0],), (contract[1],)), ((), ())),
        precision=precision,
        preferred_element_type=jnp.float32,
    )


exact_dot = functools.partial(dot, precision=lax.Precision.HIGHEST)


def split(x):
    high = x.astype(jnp.bfloat16)
    return high, (x - high.astype(jnp.float32)).astype(jnp.bfloat16)


def split_dot(x, y, contract=(1, 0)):
    rows = x[0].shape[0]
    both = dot(jnp.concatenate(x, axis=0), y[0], contract)
    return both[:rows] + (both[rows:] + dot(x[0], y[1], contract))


def identity_mask(rank):
    rows = lax.broadcasted_iota(jnp.int32, (rank, rank), 0)
    return rows == lax.broadcasted_iota(jnp.int32, (rank, rank), 1)


def mttkrp(factor, columns_c, high_ref, low_ref, ready=None):
    rank = factor.shape[0]
    both, cross = None, None
    for k in range(high_ref.shape[0]):
        if ready is not None:
            ready(k)
        high, low = split(factor * columns_c[:, k : k + 1])
        first = dot(jnp.concatenate([high, low], axis=0), high_ref[k])
        second = dot(high, low_ref[k])
        both = first if both is None else both + first
        cross = second if cross is None else cross + second
    return both[:rank] + (both[rank:] + cross)


def pack_gram(gram, width):
    rank = gram.shape[0]
    parts = width // rank
    rows = rank // parts
    return jnp.concatenate([gram[q * rows : (q + 1) * rows] for q in range(parts)], axis=1)


def pack(solved, columns_ref, high_ref, low_ref, packed_ref):
    rank, width = solved.shape
    parts = split(solved)
    packed_ref[rank:] = pack_gram(split_dot(parts, parts, (1, 1)), width)
    packed_ref[:rank] = mttkrp(solved, columns_ref[...], high_ref, low_ref)


def unpack_gram(packed, rank):
    parts = packed.shape[1] // rank
    return jnp.concatenate([packed[:, q * rank : (q + 1) * rank] for q in range(parts)], axis=0)


def tree_sum(pieces):
    pieces = list(pieces)
    while len(pieces) > 1:
        pieces = [pieces[i] + pieces[i + 1] for i in range(0, len(pieces), 2)]
    return pieces[0]


def scale_system(gram_c, gram, mask, count, normalized):
    if normalized:
        system = gram_c * gram + jnp.where(mask, gram + count * EPSILON, 0.0)
    else:
        system = gram_c * gram + jnp.where(mask, jnp.float32(count), 0.0)
    diagonal = jnp.where(mask, system, 0.0)
    row, column = [jnp.sum(diagonal, axis=axis, keepdims=True) for axis in (0, 1)]
    error = jnp.where(mask, 1.0 - RELAX, -system * (RELAX / row))
    return error, row, column


def series(error, rhs, doublings):
    power = error
    for step in range(doublings - 1):
        parts = split(power)
        rhs = rhs + split_dot(parts, split(rhs))
        power = split_dot(parts, parts) if step < doublings - 2 else dot(parts[0], parts[0])
    return rhs + dot(power.astype(jnp.bfloat16), rhs.astype(jnp.bfloat16)), power


def inverse_series(error, mask, doublings):
    total, power = jnp.where(mask, 1.0, 0.0) + error, error
    for step in range(doublings - 1):
        parts = split(power)
        power = split_dot(parts, parts) if step < doublings - 2 else dot(parts[0], parts[0])
        total = total + split_dot(split(power), split(total))
    return total, power


def careful_inverse(error, mask, total_ref, power_ref):
    unit = jnp.where(mask, 1.0, 0.0)
    system = unit - error
    bound = jnp.max(jnp.sum(jnp.abs(system), axis=0, keepdims=True), axis=1, keepdims=True)
    omega = jnp.minimum(1.0, 1.9 / bound)
    power = unit - omega * system
    total_ref[...] = unit + power
    power_ref[...] = power

    def unfinished(state):
        step, rest = state
        return jnp.logical_and(step < 48, rest > 1e-7)

    def double(state):
        power = exact_dot(power_ref[...], power_ref[...])
        power_ref[...] = power
        total = total_ref[...]
        total_ref[...] = total + exact_dot(total, power)
        return state[0] + 1, jnp.sum(power * power)

    lax.while_loop(unfinished, double, (jnp.int32(0), jnp.float32(1.0)))
    return omega * total_ref[...]


def start_kernel(tensor_hbm, factor_hbm, c_hbm, high_ref, low_ref, turned_high_ref, turned_low_ref, *refs):
    gram_c_ref, columns_ref, out_ref, tensor_ref, factor_ref, c_ref, padded_ref, sems = refs
    depth, rank = c_hbm.shape
    small = [
        pltpu.make_async_copy(c_hbm, c_ref, sems.at[depth]),
        pltpu.make_async_copy(factor_hbm, factor_ref, sems.at[depth + 1]),
    ]
    slices = []
    for k in range(0, depth, GROUP):
        some = pl.ds(k, min(GROUP, depth - k))
        slices.append(pltpu.make_async_copy(tensor_hbm.at[some], tensor_ref.at[some], sems.at[k]))
    for copy in small + slices:
        copy.start()
    for copy in small:
        copy.wait()
    padded_ref[:depth, :rank] = c_ref[...]
    columns_c = padded_ref[...].T[:rank, :depth]
    columns_ref[...] = columns_c
    factor = factor_ref[...]

    def arrive(k):
        if k % GROUP == 0 and k < depth:
            slices[k // GROUP].wait()
            for k in range(k, min(k + GROUP, depth)):
                high, low = split(tensor_ref[k])
                high_ref[k], low_ref[k] = high, low
                turned_high_ref[k], turned_low_ref[k] = high.T, low.T

    def ready(k):
        if k == 0:
            arrive(0)
        arrive(k + GROUP)
        if k == GROUP:
            gram_c_ref[...] = exact_dot(columns_c, columns_c, (1, 1))
            parts = split(factor)
            out_ref[rank:] = pack_gram(split_dot(parts, parts, (1, 1)), factor.shape[1])

    out_ref[:rank] = mttkrp(factor, columns_c, turned_high_ref, turned_low_ref, ready)


def own_core():
    return lax.axis_index("row") % 2


def own_half(rows, core):
    return pl.ds(pl.multiple_of(core * (rows // 2), 8), rows // 2)


def traded_gram(rank, sum_ref, got_ref, half_ref, swapped_ref):
    here, got, swapped = [ref[rank:] for ref in (sum_ref, got_ref, swapped_ref)]
    first = own_core() == 0
    return (here + jnp.where(first, got, swapped)) + (jnp.where(first, swapped, got) + half_ref[rank // 2 :])


def traded_sum(rank, sum_ref, got_ref, half_ref, swapped_ref, other_ref, full_ref):
    core = own_core()
    full_ref[core] = got_ref[:rank]
    full_ref[1 - core] = swapped_ref[:rank]
    full_ref[2, own_half(rank, core)] = half_ref[: rank // 2]
    full_ref[2, own_half(rank, 1 - core)] = other_ref[...]
    return (sum_ref[:rank] + full_ref[0]) + (full_ref[1] + full_ref[2])


def merge_kernel(rank, *refs):
    pieces, (out_ref, half_ref, full_ref) = refs[:-3], refs[-3:]
    if len(pieces) == 2:
        out_ref[...] = pieces[0][...] + pieces[1][...]
    else:
        out_ref[rank:] = traded_gram(rank, *pieces[:4])
        out_ref[:rank] = traded_sum(rank, *pieces, full_ref)
    half_ref[: rank // 2] = out_ref[own_half(rank, own_core())]
    half_ref[rank // 2 :] = out_ref[rank:]


def factor_scales(gram, mask, count):
    diagonal = jnp.where(mask, gram, 0.0)
    return [jnp.sqrt(jnp.sum(diagonal, axis=axis, keepdims=True) / count + EPSILON) for axis in (0, 1)]


def invert_kernel(count, *refs):
    trades, (gram_c_ref, inverse_ref, *scales_ref), scratch = refs[:4], refs[4:-2], refs[-2:]
    rank = gram_c_ref.shape[0]
    mask = identity_mask(rank)
    gram = unpack_gram(traded_gram(rank, *trades), rank)
    error, row, column = scale_system(gram_c_ref[...], gram, mask, count, True)
    scales = factor_scales(gram, mask, count)
    if scales_ref:
        scales_ref[0][...] = scales[0]
    outer = RELAX * scales[1] / column
    total, power = inverse_series(error, mask, 4)
    inverse_ref[:rank] = outer * total
    roots = 1.0 / jnp.sqrt(column), jnp.sqrt(row)
    rest = jnp.sum(jnp.square(power * roots[0] * roots[1]))
    inverse_ref[rank:] = jnp.full((8, rank), rest, jnp.float32)

    @pl.when(jnp.logical_not(rest <= TOLERANCE))
    def _():
        symmetric = error * roots[0] * roots[1]
        inverse_ref[:rank] = (outer / roots[0]) * careful_inverse(symmetric, mask, *scratch) / roots[1]


def left_kernel(pieces_count, count, normalized, last, *refs):
    pieces, refs = refs[:pieces_count], refs[pieces_count:]
    (gram_c_ref, *parts), (packed_ref, *solved_ref), scratch = refs[:4], refs[4:-2], refs[-2:]
    rank = gram_c_ref.shape[0]
    mask = identity_mask(rank)
    summed = tree_sum([ref[...] for ref in pieces])
    gram = unpack_gram(summed[rank:], rank)
    error, row, column = scale_system(gram_c_ref[...], gram, mask, count, normalized)
    outer = RELAX / column
    if normalized:
        outer = outer * factor_scales(gram, mask, count)[1]

    def emit(solved):
        if last:
            solved_ref[0][...] = solved
        pack(solved, *parts, packed_ref)

    solved, power = series(error, summed[:rank], 4)
    emit(outer * solved)
    roots = 1.0 / jnp.sqrt(column), jnp.sqrt(row)
    rest = jnp.sum(jnp.square(power * roots[0] * roots[1]))

    @pl.when(jnp.logical_not(rest <= TOLERANCE))
    def _():
        symmetric = error * roots[0] * roots[1]
        inverse = careful_inverse(symmetric, mask, *scratch)
        emit(outer / roots[0] * exact_dot(inverse, roots[0] * summed[:rank]))


def right_kernel(last, *refs):
    trades, inverse_ref, refs, full_ref = refs[:5], refs[5], refs[6:-1], refs[-1]
    rank = inverse_ref.shape[1]
    inverse = inverse_ref[:rank]
    summed = traded_sum(rank, *trades, full_ref)

    full_ref[0] = split_dot(split(inverse), split(summed))

    @pl.when(jnp.logical_not(jnp.max(inverse_ref[rank:]) <= TOLERANCE))
    def _():
        full_ref[0] = exact_dot(inverse, summed)

    solved = full_ref[0]
    if not last:
        pack(solved, *refs)
        return
    solved_ref, squares_ref = refs
    solved_ref[...] = solved
    squares = jnp.sum(solved * solved, axis=1, keepdims=True)
    row = jnp.sum(jnp.where(identity_mask(rank), squares, 0.0), axis=0, keepdims=True)
    squares_ref[...] = jnp.concatenate([row, row], axis=1) * jnp.ones((8, 1), jnp.float32)


def result_kernel(scales_ref, solved_ref, result_ref, out_ref):
    row = scales_ref[...]
    mask = identity_mask(row.shape[1])
    result_ref[...] = solved_ref[...] / jnp.sum(jnp.where(mask, row, 0.0), axis=1, keepdims=True)
    out_ref[...] = row


def shared_sum(own_ref, got_ref, far_ref, swapped_ref):
    got, swapped, first = got_ref[...], swapped_ref[...], own_core() == 0
    return (own_ref[...] + jnp.where(first, got, swapped)) + (jnp.where(first, swapped, got) + far_ref[...])


def shared_kernel(*refs):
    refs[-1][...] = shared_sum(*refs[:-1])


def finish_kernel(count, *refs):
    pieces, (scales_a_ref, solved_ref, result_ref, scales_ref) = refs[:4], refs[4:]
    rank = solved_ref.shape[0]
    row = jnp.sqrt(shared_sum(*pieces)[0:1, :rank] / count + EPSILON)
    result_ref[...] = solved_ref[...] / jnp.sum(jnp.where(identity_mask(rank), row, 0.0), axis=1, keepdims=True)
    scales_ref[...] = jnp.concatenate([scales_a_ref[...], row], axis=0)


def call(kernel, out_shape, *args, scratch=(), **options):
    return pl.pallas_call(
        kernel,
        out_shape=out_shape,
        scratch_shapes=scratch,
        compiler_params=pltpu.CompilerParams(vmem_limit_bytes=VMEM_LIMIT),
        **options,
    )(*args)


def swap(x, axis, stride):
    return lax.ppermute(x, axis, [(d, d ^ stride) for d in range(lax.axis_size(axis))])


def exchange(x, axis, stride=1, radix=4):
    size = lax.axis_size(axis)
    while True:
        group = min(radix, size // stride)
        pieces = [x] + [swap(x, axis, m * stride) for m in range(1, group)]
        stride *= group
        if stride >= size:
            return pieces
        x = tree_sum(pieces)


def exchange_by_cores(x, axis, rank):
    size = lax.axis_size(axis)
    out = jax.ShapeDtypeStruct((x.shape[0] - rank // 2, x.shape[1]), x.dtype)
    scratch = [pltpu.VMEM((3, rank, x.shape[1]), x.dtype)]
    stride, pieces = 2, (x, swap(x, axis, 1))
    while stride < size:
        x, own = call(functools.partial(merge_kernel, rank), (x, out), *pieces, scratch=scratch)
        half = swap(own, axis, 3 * stride)
        got = lax.ppermute(x, axis, [(d, d ^ (stride if d % 2 == 0 else 2 * stride)) for d in range(size)])
        pieces = (x, got, half, swap(got, axis, 1), swap(half[: rank // 2], axis, 1))
        stride *= 4
    return pieces


def exchange_shared(x, axis, core_axis):
    size, cores, stride = lax.axis_size(axis), lax.axis_size(core_axis), 1
    while True:
        far = swap(x, axis, 3 * stride)
        pairs = [
            (d * size + e, d * size + (e ^ (stride << d % 2))) for d in range(cores) for e in range(size)
        ]
        got = lax.ppermute(x, (core_axis, axis), pairs)
        pieces = (x, got, far, swap(got, core_axis, 1))
        stride *= 4
        if stride >= size:
            return pieces
        x = call(shared_kernel, x, *pieces)


def shards(tensor, factor_b, factor_c):
    rows_all = tensor.shape[1] * lax.axis_size("row")
    cols_all = tensor.shape[2] * lax.axis_size("col")
    depth, height, width = tensor.shape
    rank = factor_c.shape[1]
    f32 = functools.partial(jax.ShapeDtypeStruct, dtype=jnp.float32)
    part = jax.ShapeDtypeStruct(tensor.shape, jnp.bfloat16)
    turned = jax.ShapeDtypeStruct((depth, width, height), jnp.bfloat16)
    left, right = (rank, height), (rank, width)
    packed_a, packed_b = [(rank + rank * rank // n, n) for n in (height, width)]
    scratch = [pltpu.VMEM((rank, rank), jnp.float32)] * 2
    full = [pltpu.VMEM((3, rank, width), jnp.float32)]
    high, low, turned_high, turned_low, gram_c, columns, partial = call(
        start_kernel,
        (part, part, turned, turned, f32((rank, rank)), f32((rank, depth)), f32(packed_a)),
        *[pltpu.with_memory_space_constraint(x, pltpu.HBM) for x in (tensor, factor_b, factor_c)],
        in_specs=[pl.BlockSpec(memory_space=pltpu.HBM)] * 3,
        scratch=[
            pltpu.VMEM(tensor.shape, jnp.float32),
            pltpu.VMEM(factor_b.shape, jnp.float32),
            pltpu.VMEM(factor_c.shape, jnp.float32),
            pltpu.VMEM((128, 128), jnp.float32),
            pltpu.SemaphoreType.DMA((depth + 2,)),
        ],
    )
    cost = pl.CostEstimate(flops=0, bytes_accessed=4 * tensor.size, transcendentals=0)
    for sweep in range(SWEEPS):
        last = sweep == SWEEPS - 1
        pieces = exchange(partial, "col")
        kernel = functools.partial(left_kernel, len(pieces), cols_all, sweep > 0, last)
        outs = (f32(packed_b), f32(left)) if last else (f32(packed_b),)
        partial, *solved_a = call(kernel, outs, *pieces, gram_c, columns, high, low, scratch=scratch)
        pieces = exchange_by_cores(partial, "row", rank)
        kernel = functools.partial(invert_kernel, rows_all)
        outs = (f32((rank + 8, rank)), f32((1, rank))) if last else (f32((rank + 8, rank)),)
        inverse, *scales_a = call(kernel, outs, *pieces[:4], gram_c, scratch=scratch, cost_estimate=cost)
        kernel = functools.partial(right_kernel, last)
        if not last:
            partial = call(
                kernel, f32(packed_a), *pieces, inverse, columns, turned_high, turned_low, scratch=full
            )
        else:
            solved_b, squares = call(kernel, (f32(right), f32((8, 2 * rank))), *pieces, inverse, scratch=full)
    pieces = exchange_shared(squares, "col", "row")
    result_a, scales_a = call(result_kernel, (f32(left), f32((1, rank))), *scales_a, *solved_a, cost_estimate=cost)
    kernel = functools.partial(finish_kernel, cols_all)
    result_b, scales = call(kernel, (f32(right), f32((2, rank))), *pieces, scales_a, solved_b)
    return result_a, result_b, scales


def solution(mesh):
    in_specs = (P(None, "row", "col"), P(None, "col"), P())
    out_specs = (P(None, "row"), P(None, "col"), P())
    return jax.shard_map(shards, mesh=mesh, in_specs=in_specs, out_specs=out_specs, check_vma=False)
```

```python
import functools

import jax
import jax.numpy as jnp
from jax import lax
from jax.experimental import pallas as pl
from jax.experimental.pallas import tpu as pltpu
from jax.sharding import PartitionSpec as P

SWEEPS = 3
EPSILON = 1e-06
TOLERANCE = 2e-06
RELAX = 0.95
GROUP = 4
VMEM_LIMIT = 16 * 1024 * 1024


def dot(x, y, contract=(1, 0), precision=None):
    return lax.dot_general(
        x,
        y,
        (((contract[0],), (contract[1],)), ((), ())),
        precision=precision,
        preferred_element_type=jnp.float32,
    )


exact_dot = functools.partial(dot, precision=lax.Precision.HIGHEST)


def split(x):
    high = x.astype(jnp.bfloat16)
    return high, (x - high.astype(jnp.float32)).astype(jnp.bfloat16)


def split_dot(x, y, contract=(1, 0)):
    rows = x[0].shape[0]
    both = dot(jnp.concatenate(x, axis=0), y[0], contract)
    return both[:rows] + (both[rows:] + dot(x[0], y[1], contract))


def identity_mask(rank):
    rows = lax.broadcasted_iota(jnp.int32, (rank, rank), 0)
    return rows == lax.broadcasted_iota(jnp.int32, (rank, rank), 1)


def mttkrp(factor, wide_ref, high_ref, low_ref, ready=None):
    rank = factor.shape[0]
    both, cross = None, None
    for k in range(high_ref.shape[0]):
        if ready is not None:
            ready(k)
        spread = wide_ref[k]
        high, low = split(factor * jnp.concatenate([spread] * (factor.shape[1] // spread.shape[1]), axis=1))
        first = dot(jnp.concatenate([high, low], axis=0), high_ref[k])
        second = dot(high, low_ref[k])
        both = first if both is None else both + first
        cross = second if cross is None else cross + second
    return both[:rank] + (both[rank:] + cross)


def pack_gram(gram, width):
    rank = gram.shape[0]
    parts = width // rank
    rows = rank // parts
    return jnp.concatenate([gram[q * rows : (q + 1) * rows] for q in range(parts)], axis=1)


def pack(solved, wide_ref, high_ref, low_ref, packed_ref):
    rank, width = solved.shape
    parts = split(solved)
    packed_ref[rank:] = pack_gram(split_dot(parts, parts, (1, 1)), width)
    packed_ref[:rank] = mttkrp(solved, wide_ref, high_ref, low_ref)


def unpack_gram(packed, rank):
    parts = packed.shape[1] // rank
    return jnp.concatenate([packed[:, q * rank : (q + 1) * rank] for q in range(parts)], axis=0)


def tree_sum(pieces):
    pieces = list(pieces)
    while len(pieces) > 1:
        pieces = [pieces[i] + pieces[i + 1] for i in range(0, len(pieces), 2)]
    return pieces[0]


def scale_system(gram_c, gram, mask, count, normalized):
    if normalized:
        system = gram_c * gram + jnp.where(mask, gram + count * EPSILON, 0.0)
    else:
        system = gram_c * gram + jnp.where(mask, jnp.float32(count), 0.0)
    diagonal = jnp.where(mask, system, 0.0)
    row, column = [jnp.sum(diagonal, axis=axis, keepdims=True) for axis in (0, 1)]
    error = jnp.where(mask, 1.0 - RELAX, -system * (RELAX / row))
    return error, row, column


def series(error, rhs, doublings):
    power = error
    for step in range(doublings - 1):
        parts = split(power)
        rhs = rhs + split_dot(parts, split(rhs))
        power = split_dot(parts, parts) if step < doublings - 2 else dot(parts[0], parts[0])
    return rhs + dot(power.astype(jnp.bfloat16), rhs.astype(jnp.bfloat16)), power


def inverse_series(error, mask, doublings):
    total, power = jnp.where(mask, 1.0, 0.0) + error, error
    for step in range(doublings - 1):
        parts = split(power)
        power = split_dot(parts, parts) if step < doublings - 2 else dot(parts[0], parts[0])
        total = total + split_dot(split(power), split(total))
    return total, power


def careful_inverse(error, mask, total_ref, power_ref):
    unit = jnp.where(mask, 1.0, 0.0)
    system = unit - error
    bound = jnp.max(jnp.sum(jnp.abs(system), axis=0, keepdims=True), axis=1, keepdims=True)
    omega = jnp.minimum(1.0, 1.9 / bound)
    power = unit - omega * system
    total_ref[...] = unit + power
    power_ref[...] = power

    def unfinished(state):
        step, rest = state
        return jnp.logical_and(step < 48, rest > 1e-7)

    def double(state):
        power = exact_dot(power_ref[...], power_ref[...])
        power_ref[...] = power
        total = total_ref[...]
        total_ref[...] = total + exact_dot(total, power)
        return state[0] + 1, jnp.sum(power * power)

    lax.while_loop(unfinished, double, (jnp.int32(0), jnp.float32(1.0)))
    return omega * total_ref[...]


def start_kernel(tensor_hbm, factor_hbm, c_hbm, high_ref, low_ref, turned_high_ref, turned_low_ref, *refs):
    gram_c_ref, wide_ref, out_ref, tensor_ref, factor_ref, c_ref, padded_ref, sems = refs
    depth, rank = c_hbm.shape
    small = [
        pltpu.make_async_copy(c_hbm, c_ref, sems.at[depth]),
        pltpu.make_async_copy(factor_hbm, factor_ref, sems.at[depth + 1]),
    ]
    slices = []
    for k in range(0, depth, GROUP):
        some = pl.ds(k, min(GROUP, depth - k))
        slices.append(pltpu.make_async_copy(tensor_hbm.at[some], tensor_ref.at[some], sems.at[k]))
    for copy in small + slices:
        copy.start()
    for copy in small:
        copy.wait()
    padded_ref[:depth, :rank] = c_ref[...]
    columns_c = padded_ref[...].T[:rank, :depth]
    for k in range(depth):
        wide_ref[k] = jnp.broadcast_to(columns_c[:, k : k + 1], wide_ref.shape[1:])
    factor = factor_ref[...]

    def arrive(k):
        if k % GROUP == 0 and k < depth:
            slices[k // GROUP].wait()
            for k in range(k, min(k + GROUP, depth)):
                high, low = split(tensor_ref[k])
                high_ref[k], low_ref[k] = high, low
                turned_high_ref[k], turned_low_ref[k] = high.T, low.T

    def ready(k):
        if k == 0:
            arrive(0)
        arrive(k + GROUP)
        if k == GROUP:
            gram_c_ref[...] = exact_dot(columns_c, columns_c, (1, 1))
            parts = split(factor)
            out_ref[rank:] = pack_gram(split_dot(parts, parts, (1, 1)), factor.shape[1])

    out_ref[:rank] = mttkrp(factor, wide_ref, turned_high_ref, turned_low_ref, ready)


def own_core():
    return lax.axis_index("row") % 2


def own_half(rows, core):
    return pl.ds(pl.multiple_of(core * (rows // 2), 8), rows // 2)


def traded_gram(rank, sum_ref, got_ref, half_ref, swapped_ref):
    here, got, swapped = [ref[rank:] for ref in (sum_ref, got_ref, swapped_ref)]
    first = own_core() == 0
    return (here + jnp.where(first, got, swapped)) + (jnp.where(first, swapped, got) + half_ref[rank // 2 :])


def traded_sum(rank, sum_ref, got_ref, half_ref, swapped_ref, other_ref, full_ref):
    core = own_core()
    full_ref[core] = got_ref[:rank]
    full_ref[1 - core] = swapped_ref[:rank]
    full_ref[2, own_half(rank, core)] = half_ref[: rank // 2]
    full_ref[2, own_half(rank, 1 - core)] = other_ref[...]
    return (sum_ref[:rank] + full_ref[0]) + (full_ref[1] + full_ref[2])


def merge_kernel(rank, *refs):
    pieces, (out_ref, half_ref, full_ref) = refs[:-3], refs[-3:]
    if len(pieces) == 2:
        out_ref[...] = pieces[0][...] + pieces[1][...]
    else:
        out_ref[rank:] = traded_gram(rank, *pieces[:4])
        out_ref[:rank] = traded_sum(rank, *pieces, full_ref)
    half_ref[: rank // 2] = out_ref[own_half(rank, own_core())]
    half_ref[rank // 2 :] = out_ref[rank:]


def factor_scales(gram, mask, count):
    diagonal = jnp.where(mask, gram, 0.0)
    return [jnp.sqrt(jnp.sum(diagonal, axis=axis, keepdims=True) / count + EPSILON) for axis in (0, 1)]


def invert_kernel(count, *refs):
    trades, (gram_c_ref, inverse_ref, *scales_ref), scratch = refs[:4], refs[4:-2], refs[-2:]
    rank = gram_c_ref.shape[0]
    mask = identity_mask(rank)
    gram = unpack_gram(traded_gram(rank, *trades), rank)
    error, row, column = scale_system(gram_c_ref[...], gram, mask, count, True)
    scales = factor_scales(gram, mask, count)
    if scales_ref:
        scales_ref[0][...] = scales[0]
    outer = RELAX * scales[1] / column
    total, power = inverse_series(error, mask, 4)
    inverse_ref[:rank] = outer * total
    roots = 1.0 / jnp.sqrt(column), jnp.sqrt(row)
    rest = jnp.sum(jnp.square(power * roots[0] * roots[1]))
    inverse_ref[rank:] = jnp.full((8, rank), rest, jnp.float32)

    @pl.when(jnp.logical_not(rest <= TOLERANCE))
    def _():
        symmetric = error * roots[0] * roots[1]
        inverse_ref[:rank] = (outer / roots[0]) * careful_inverse(symmetric, mask, *scratch) / roots[1]


def left_kernel(pieces_count, count, normalized, last, *refs):
    pieces, refs = refs[:pieces_count], refs[pieces_count:]
    (gram_c_ref, *parts), (packed_ref, *solved_ref), scratch = refs[:4], refs[4:-2], refs[-2:]
    rank = gram_c_ref.shape[0]
    mask = identity_mask(rank)
    summed = tree_sum([ref[...] for ref in pieces])
    gram = unpack_gram(summed[rank:], rank)
    error, row, column = scale_system(gram_c_ref[...], gram, mask, count, normalized)
    outer = RELAX / column
    if normalized:
        outer = outer * factor_scales(gram, mask, count)[1]

    def emit(solved):
        if last:
            solved_ref[0][...] = solved
        pack(solved, *parts, packed_ref)

    solved, power = series(error, summed[:rank], 4)
    emit(outer * solved)
    roots = 1.0 / jnp.sqrt(column), jnp.sqrt(row)
    rest = jnp.sum(jnp.square(power * roots[0] * roots[1]))

    @pl.when(jnp.logical_not(rest <= TOLERANCE))
    def _():
        symmetric = error * roots[0] * roots[1]
        inverse = careful_inverse(symmetric, mask, *scratch)
        emit(outer / roots[0] * exact_dot(inverse, roots[0] * summed[:rank]))


def right_kernel(last, *refs):
    trades, inverse_ref, refs, full_ref = refs[:5], refs[5], refs[6:-1], refs[-1]
    rank = inverse_ref.shape[1]
    inverse = inverse_ref[:rank]
    summed = traded_sum(rank, *trades, full_ref)

    full_ref[0] = split_dot(split(inverse), split(summed))

    @pl.when(jnp.logical_not(jnp.max(inverse_ref[rank:]) <= TOLERANCE))
    def _():
        full_ref[0] = exact_dot(inverse, summed)

    solved = full_ref[0]
    if not last:
        pack(solved, *refs)
        return
    solved_ref, squares_ref = refs
    solved_ref[...] = solved
    squares = jnp.sum(solved * solved, axis=1, keepdims=True)
    row = jnp.sum(jnp.where(identity_mask(rank), squares, 0.0), axis=0, keepdims=True)
    squares_ref[...] = jnp.concatenate([row, row], axis=1) * jnp.ones((8, 1), jnp.float32)


def result_kernel(scales_ref, solved_ref, result_ref, out_ref):
    row = scales_ref[...]
    mask = identity_mask(row.shape[1])
    result_ref[...] = solved_ref[...] / jnp.sum(jnp.where(mask, row, 0.0), axis=1, keepdims=True)
    out_ref[...] = row


def shared_sum(own_ref, got_ref, far_ref, swapped_ref):
    got, swapped, first = got_ref[...], swapped_ref[...], own_core() == 0
    return (own_ref[...] + jnp.where(first, got, swapped)) + (jnp.where(first, swapped, got) + far_ref[...])


def shared_kernel(*refs):
    refs[-1][...] = shared_sum(*refs[:-1])


def finish_kernel(count, *refs):
    pieces, (scales_a_ref, solved_ref, result_ref, scales_ref) = refs[:4], refs[4:]
    rank = solved_ref.shape[0]
    row = jnp.sqrt(shared_sum(*pieces)[0:1, :rank] / count + EPSILON)
    result_ref[...] = solved_ref[...] / jnp.sum(jnp.where(identity_mask(rank), row, 0.0), axis=1, keepdims=True)
    scales_ref[...] = jnp.concatenate([scales_a_ref[...], row], axis=0)


def call(kernel, out_shape, *args, scratch=(), **options):
    return pl.pallas_call(
        kernel,
        out_shape=out_shape,
        scratch_shapes=scratch,
        compiler_params=pltpu.CompilerParams(vmem_limit_bytes=VMEM_LIMIT),
        **options,
    )(*args)


def swap(x, axis, stride):
    return lax.ppermute(x, axis, [(d, d ^ stride) for d in range(lax.axis_size(axis))])


def exchange(x, axis, stride=1, radix=4):
    size = lax.axis_size(axis)
    while True:
        group = min(radix, size // stride)
        pieces = [x] + [swap(x, axis, m * stride) for m in range(1, group)]
        stride *= group
        if stride >= size:
            return pieces
        x = tree_sum(pieces)


def exchange_by_cores(x, axis, rank):
    size = lax.axis_size(axis)
    out = jax.ShapeDtypeStruct((x.shape[0] - rank // 2, x.shape[1]), x.dtype)
    scratch = [pltpu.VMEM((3, rank, x.shape[1]), x.dtype)]
    stride, pieces = 2, (x, swap(x, axis, 1))
    while stride < size:
        x, own = call(functools.partial(merge_kernel, rank), (x, out), *pieces, scratch=scratch)
        half = swap(own, axis, 3 * stride)
        got = lax.ppermute(x, axis, [(d, d ^ (stride if d % 2 == 0 else 2 * stride)) for d in range(size)])
        pieces = (x, got, half, swap(got, axis, 1), swap(half[: rank // 2], axis, 1))
        stride *= 4
    return pieces


def exchange_shared(x, axis, core_axis):
    size, cores, stride = lax.axis_size(axis), lax.axis_size(core_axis), 1
    while True:
        far = swap(x, axis, 3 * stride)
        pairs = [
            (d * size + e, d * size + (e ^ (stride << d % 2))) for d in range(cores) for e in range(size)
        ]
        got = lax.ppermute(x, (core_axis, axis), pairs)
        pieces = (x, got, far, swap(got, core_axis, 1))
        stride *= 4
        if stride >= size:
            return pieces
        x = call(shared_kernel, x, *pieces)


def shards(tensor, factor_b, factor_c):
    rows_all = tensor.shape[1] * lax.axis_size("row")
    cols_all = tensor.shape[2] * lax.axis_size("col")
    depth, height, width = tensor.shape
    rank = factor_c.shape[1]
    f32 = functools.partial(jax.ShapeDtypeStruct, dtype=jnp.float32)
    part = jax.ShapeDtypeStruct(tensor.shape, jnp.bfloat16)
    turned = jax.ShapeDtypeStruct((depth, width, height), jnp.bfloat16)
    left, right = (rank, height), (rank, width)
    packed_a, packed_b = [(rank + rank * rank // n, n) for n in (height, width)]
    scratch = [pltpu.VMEM((rank, rank), jnp.float32)] * 2
    full = [pltpu.VMEM((3, rank, width), jnp.float32)]
    high, low, turned_high, turned_low, gram_c, wide, partial = call(
        start_kernel,
        (part, part, turned, turned, f32((rank, rank)), f32((depth, rank, 128)), f32(packed_a)),
        *[pltpu.with_memory_space_constraint(x, pltpu.HBM) for x in (tensor, factor_b, factor_c)],
        in_specs=[pl.BlockSpec(memory_space=pltpu.HBM)] * 3,
        scratch=[
            pltpu.VMEM(tensor.shape, jnp.float32),
            pltpu.VMEM(factor_b.shape, jnp.float32),
            pltpu.VMEM(factor_c.shape, jnp.float32),
            pltpu.VMEM((128, 128), jnp.float32),
            pltpu.SemaphoreType.DMA((depth + 2,)),
        ],
    )
    cost = pl.CostEstimate(flops=0, bytes_accessed=4 * tensor.size, transcendentals=0)
    for sweep in range(SWEEPS):
        last = sweep == SWEEPS - 1
        pieces = exchange(partial, "col")
        kernel = functools.partial(left_kernel, len(pieces), cols_all, sweep > 0, last)
        outs = (f32(packed_b), f32(left)) if last else (f32(packed_b),)
        partial, *solved_a = call(kernel, outs, *pieces, gram_c, wide, high, low, scratch=scratch)
        pieces = exchange_by_cores(partial, "row", rank)
        kernel = functools.partial(invert_kernel, rows_all)
        outs = (f32((rank + 8, rank)), f32((1, rank))) if last else (f32((rank + 8, rank)),)
        inverse, *scales_a = call(kernel, outs, *pieces[:4], gram_c, scratch=scratch, cost_estimate=cost)
        kernel = functools.partial(right_kernel, last)
        if not last:
            partial = call(
                kernel, f32(packed_a), *pieces, inverse, wide, turned_high, turned_low, scratch=full
            )
        else:
            solved_b, squares = call(kernel, (f32(right), f32((8, 2 * rank))), *pieces, inverse, scratch=full)
    pieces = exchange_shared(squares, "col", "row")
    result_a, scales_a = call(result_kernel, (f32(left), f32((1, rank))), *scales_a, *solved_a, cost_estimate=cost)
    kernel = functools.partial(finish_kernel, cols_all)
    result_b, scales = call(kernel, (f32(right), f32((2, rank))), *pieces, scales_a, solved_b)
    return result_a, result_b, scales


def solution(mesh):
    in_specs = (P(None, "row", "col"), P(None, "col"), P())
    out_specs = (P(None, "row"), P(None, "col"), P())
    return jax.shard_map(shards, mesh=mesh, in_specs=in_specs, out_specs=out_specs, check_vma=False)
```
